256 devices in a mesh: attn: 8 (over z), expert: 32 (over y, x, core).
Axes of the slice: x: 4, y: 4, z: 8, core: 2. Of those that a mesh axis runs over, the one named last changes fastest.
Arguments:
- tokens: bfloat16 [512, 7168], P(('attn', 'expert')), may hold values from -6 to 6
- expert_ids: int32 [512, 8], P(('attn', 'expert')), may hold values from 0 to 31, all different within a row; in each aligned block of 64 rows (0 to 63, 64 to 127, ...) at most 24 rows name the same one
- replica: int32 [512, 8], P(('attn', 'expert')), may hold values from 0 to 1
- route_weight: float32 [512, 8], P(('attn', 'expert')), may hold values from 0.05 to 0.5
- spare_plan: int32 [32], replicated, may hold values from 0 to 31, each once
- w_in: bfloat16 [32, 2, 7168, 1024], P('expert', None, None, 'attn'), may hold values from -0.0625 to 0.0625
- w_down: bfloat16 [32, 1024, 7168], P('expert', 'attn'), may hold values from -0.1875 to 0.1875
Outputs:
- layer_output: bfloat16 [512, 7168], P(('attn', 'expert'))
- slot_load: int32 [32, 2], P('expert')
The draws below stay inside these ranges and needn't reach their ends.
Inputs may be any that keep to these rules, and one draw needn't show every extreme that they name: `expert_ids`: each row names 8 different experts; among the rows of one index of attn no expert is named by more than 24 rows, and one is named by exactly 24. `replica`: 0 names the expert's own index of expert, 1 the index whose spare slot holds it. `spare_plan`: each expert appears once.
All inputs are finite; a program needn't handle non-finite values.
Results may differ from the reference program's by a relative error of at most 0.023.
Values may be sent and summed in bfloat16 or wider, within the bound.
No kernel may reach another device: no remote copies, remote signals or barrier semaphores. Data moves between devices by JAX's collectives and lax.ppermute only.
A program may use at most 128 MiB of HBM per device.

```python
import math
import jax
import jax.numpy as jnp
import numpy as np
from jax import lax

D = 7168
FF = 1024
TOP = 8
ROWS_DEV = 2
EXPERTS = 32
TOKENS = 512
MOST = 24
N_ATTN = 8
N_EXPERT = 32


def set_ends(entries, stream_key, smallest, largest):
    longest = entries.shape.index(max(entries.shape))
    spots = []
    for shift in (0, 1):
        where = [jax.random.randint(jax.random.fold_in(stream_key, axis), (), 0, length) for axis, length in enumerate(entries.shape)]
        where[longest] = (where[longest] + shift) % entries.shape[longest]
        spots.append(tuple(where))
    return entries.at[spots[0]].set(smallest).at[spots[1]].set(largest)


def levels(own_key, extent, shards, low, largest):
    factor_of, own = 1.0, jax.random.fold_in(own_key, 6)
    for axis_at, blocks in shards:
        draws = jnp.exp(jax.random.uniform(jax.random.fold_in(own, axis_at), (blocks,), jnp.float32, low / len(shards), largest / len(shards)))
        factor_of = factor_of * jnp.repeat(draws, extent[axis_at] // blocks).reshape([-1 if axis == axis_at else 1 for axis in range(len(extent))])
    return factor_of


def assign_block(key, own, number, rows, count, top, most, slope):
    order = jax.random.permutation(key, count)
    crowded, usual = load_shares(count, rows * top, most, slope, True), load_shares(count, rows * top, most, slope, False)
    places = jnp.arange(count)

    def named(lengths, rotation):
        used = int((lengths > 0).sum())
        fixed = max(1, used // 4)
        shifted = fixed + (places - fixed + rotation * (used - fixed)) % max(1, count - fixed)
        return jnp.zeros((count,), jnp.int32).at[order[jnp.where(places < fixed, places, shifted)]].set(jnp.asarray(lengths, jnp.int32))

    lengths = jnp.where(number % 4 == 0, named(crowded, number // 4), named(usual, number - number // 4 - 1))
    mixed = jax.random.permutation(jax.random.fold_in(own, 3), count)
    source_of, receiver = mixed[0:count // 2 * 2:2], mixed[1:count // 2 * 2:2]
    slack = jnp.minimum(lengths[source_of] - 1, most - lengths[receiver]) // 2
    slack = jnp.where((source_of == order[0]) | (receiver == order[0]) | (lengths[receiver] == 0), 0, jnp.maximum(slack, 0))
    shifted = jax.random.randint(jax.random.fold_in(own, 4), (count // 2,), 0, 1 << 20) % (slack + 1)
    lengths = lengths.at[source_of].add(-shifted).at[receiver].add(shifted)
    items = jnp.searchsorted(jnp.cumsum(lengths), jnp.arange(rows * top), side="right").astype(jnp.int32)
    table = items.reshape(top, rows).T
    table = table[jax.random.permutation(jax.random.fold_in(own, 1), rows)]
    rotation = jax.random.randint(jax.random.fold_in(own, 2), (rows, 1), 0, top)
    return jnp.take_along_axis(table, (jnp.arange(top)[None, :] + rotation) % top, axis=1)


def load_shares(count, total, most, slope, full):
    weights = [(1 << 20) // math.isqrt(grade ** slope) + 1 for grade in range(1, count + 1)]
    largest = most if full else min(most, max(-(-total // count), total * weights[0] // sum(weights)))
    least = 1 if total - largest >= count - 1 else 0
    counts, spare = [largest] + [least] * (count - 1), total - largest - least * (count - 1)
    while spare > 0:
        movable = [i for i in range(1, count) if counts[i] < largest] or [i for i in range(1, count) if counts[i] < most]
        mass, left = sum([weights[i] for i in movable]), spare
        for i in movable:
            extra = min(most - counts[i], max(1, left * weights[i] // mass), spare)
            counts[i] = counts[i] + extra
            spare = spare - extra
    return np.array(counts)


def bell_draw(rng, dims, deviation, limit, cuts=(), held_as=jnp.bfloat16):
    result = jax.random.normal(rng, dims, jnp.float32) * deviation
    if len(cuts) > 0:
        result = levels(rng, dims, cuts, -0.22, 0.18) * result
    return jnp.clip(result, min=-limit, max=limit).astype(held_as)


def setup_inputs(seed: int = 0) -> dict:
    key_list = jax.random.split(jax.random.key(seed), 8)
    tokens = bell_draw(key_list[0], (TOKENS, D), 1.0, 6.0, ((0, 256),))
    expert_ids_keys = jax.random.split(jax.random.fold_in(key_list[1], 1), TOKENS // (ROWS_DEV * N_EXPERT))
    expert_ids_turns = jax.random.permutation(jax.random.fold_in(key_list[1], 3), TOKENS // (ROWS_DEV * N_EXPERT))
    expert_ids = jax.vmap(lambda own, number: assign_block(jax.random.fold_in(key_list[1], 2), own, number, ROWS_DEV * N_EXPERT, EXPERTS, TOP, MOST, 2))(expert_ids_keys, expert_ids_turns).reshape((TOKENS, TOP))
    replica = set_ends(jax.random.randint(key_list[2], (TOKENS, TOP), 0, 2), jax.random.fold_in(key_list[2], 1), 0, 1).astype(jnp.int32)
    route_weight = jnp.clip(jnp.exp(math.log(0.5) - 2.3025851 * jax.random.uniform(key_list[3], (TOKENS, TOP), jnp.float32) ** levels(key_list[3], (TOKENS, TOP), ((0, 256),), -0.2, 0.2)), 0.05, 0.5)
    spare_plan = jax.random.permutation(key_list[4], EXPERTS).astype(jnp.int32)
    w_in = bell_draw(key_list[5], (EXPERTS, 2, D, FF), D ** -0.5, 0.0625, ((0, 32), (3, 8)))
    w_down = bell_draw(key_list[6], (EXPERTS, FF, D), FF ** -0.5, 0.1875, ((0, 32), (1, 8)))
    return dict(tokens=tokens, expert_ids=expert_ids, replica=replica, route_weight=route_weight, spare_plan=spare_plan, w_in=w_in, w_down=w_down)


def reference(tokens, expert_ids, replica, route_weight, spare_plan, w_in, w_down):
    capacity = N_ATTN * MOST
    block_width = FF // N_ATTN

    def one_expert(expert, total):
        matches = expert_ids == expert
        coefficient = jnp.sum(matches.astype(jnp.float32) * route_weight, 1)
        flagged = jnp.any(matches, 1).astype(jnp.int32)
        ordering = jnp.argsort(1 - flagged, stable=True)[:capacity].astype(jnp.int32)
        chosen = tokens[ordering]
        weights_in = lax.dynamic_index_in_dim(w_in, expert, 0, keepdims=False)
        weights_down = lax.dynamic_index_in_dim(w_down, expert, 0, keepdims=False)
        gate_part = jnp.dot(chosen, weights_in[0], preferred_element_type=jnp.float32)
        up_part = jnp.dot(chosen, weights_in[1], preferred_element_type=jnp.float32)
        hidden = (jax.nn.silu(gate_part) * up_part).astype(jnp.bfloat16)
        hidden_blocks = hidden.reshape(capacity, N_ATTN, block_width).astype(jnp.float32)
        down_blocks = weights_down.reshape(N_ATTN, block_width, D).astype(jnp.float32)
        partial_value = jnp.einsum('caf,afd->acd', hidden_blocks, down_blocks).astype(jnp.bfloat16)
        partial_value = lax.optimization_barrier(partial_value)
        expert_out = jnp.sum(partial_value.astype(jnp.float32), 0).astype(jnp.bfloat16)
        weighted = coefficient[ordering][:, None] * expert_out.astype(jnp.float32)
        return total.at[ordering].add(weighted)

    total = lax.fori_loop(0, EXPERTS, one_expert, jnp.zeros((TOKENS, D), jnp.float32))
    layer_output = total.astype(jnp.bfloat16)

    labels = jnp.arange(EXPERTS, dtype=jnp.int32)
    named = expert_ids[..., None] == labels
    by_owner = jnp.sum(named & (replica == 0)[..., None], axis=(0, 1), dtype=jnp.int32)
    by_copy = jnp.sum(named & (replica == 1)[..., None], axis=(0, 1), dtype=jnp.int32)
    by_spare = by_copy[spare_plan]
    slot_load = jnp.stack([by_owner, by_spare], 1).astype(jnp.int32)
    return layer_output, slot_load
```

```python
import jax
import jax.numpy as jnp
from jax import lax
from jax.sharding import PartitionSpec as P

F32, BF16 = jnp.float32, jnp.bfloat16
MOST = 24
META = 128


def ring_shift(value, step, count):
    return lax.ppermute(value, "attn", [(i, (i + step) % count) for i in range(count)])


def core_swap(value, groups):
    return lax.ppermute(value, "expert", [(i, i ^ 1) for i in range(groups)])


def gather_ring(chunks, count):
    half = count // 2
    right = [[c] for c in chunks]
    left = [[c] for c in chunks]
    for step in range(half):
        for r, l in zip(right, left):
            r.append(ring_shift(r[-1], 1, count))
            if step < half - 1:
                l.append(ring_shift(l[-1], count - 1, count))
    return [r + l[1:] for r, l in zip(right, left)]


def reduce_ring(chunks, count):
    half = count // 2
    right = [f(half).astype(BF16) for f in chunks]
    left = [f(count - half + 1).astype(BF16) for f in chunks]
    for step in range(half - 1, 0, -1):
        for c, f in enumerate(chunks):
            right[c] = (ring_shift(right[c], 1, count).astype(F32) + f(step)).astype(BF16)
            if step > 1:
                left[c] = (
                    ring_shift(left[c], count - 1, count).astype(F32) + f(count - step + 1)
                ).astype(BF16)
    return [
        (
            f(0)
            + ring_shift(right[c], 1, count).astype(F32)
            + ring_shift(left[c], count - 1, count).astype(F32)
        ).astype(BF16)
        for c, f in enumerate(chunks)
    ]


def body(tokens, expert_ids, replica, route_weight, spare_plan, w_in, w_down):
    rows, width = tokens.shape
    top = expert_ids.shape[1]
    count = lax.axis_size("attn")
    groups = lax.axis_size("expert")
    me = lax.axis_index("expert")
    peers = groups // 2
    same_core = [[core + 2 * j for j in range(peers)] for core in range(2)]

    high = route_weight.astype(BF16)
    rest = route_weight - high.astype(F32)
    middle = rest.astype(BF16)
    low = (rest - middle.astype(F32)).astype(BF16)
    meta = [expert_ids.astype(BF16), replica.astype(BF16), high, middle, low]
    pad = jnp.zeros((rows, META - 5 * top), BF16)
    sent = jnp.concatenate([tokens] + meta + [pad], 1)

    spread = jnp.broadcast_to(sent[None], (peers, rows, width + META))
    near = lax.all_to_all(spread, "expert", 0, 0, axis_index_groups=same_core, tiled=True)
    near = near.reshape(peers * rows, width + META)
    far = core_swap(near, groups)
    group_rows = jnp.concatenate([near, far], 0)
    total = group_rows.shape[0]

    info = group_rows[:, width : width + 5 * top].astype(F32).reshape(total, 5, top)
    ids, copies = info[:, 0], info[:, 1]
    weights = info[:, 2] + info[:, 3] + info[:, 4]
    named = ids == me.astype(F32)
    spare = lax.dynamic_index_in_dim(spare_plan, me, 0, keepdims=False).astype(F32)
    counts = jnp.stack(
        [
            jnp.sum((named & (copies == 0.0)).astype(F32)),
            jnp.sum(((ids == spare) & (copies == 1.0)).astype(F32)),
        ]
    )
    hit = jnp.sum(named.astype(F32), 1)
    coef = jnp.sum(jnp.where(named, weights, 0.0), 1)
    place = jnp.arange(total, dtype=jnp.int32)
    before = (place[:, None] > place[None, :]).astype(F32)
    rank = jnp.sum(before * hit[None, :], 1)
    slot = jnp.arange(MOST, dtype=jnp.int32).astype(F32)
    chosen = jnp.where((hit[None, :] > 0.0) & (rank[None, :] == slot[:, None]), 1.0, 0.0)
    packed = jnp.dot(chosen.astype(BF16), group_rows[:, :width], preferred_element_type=F32)
    packed = packed.astype(BF16)
    half = width // 2
    tail = jnp.broadcast_to(jnp.pad(counts, (0, META - 2))[None], (MOST, META)).astype(BF16)
    parts = [jnp.concatenate([packed[:, :half], tail], 1), packed[:, half:]]
    first, second = gather_ring(parts, count)

    load = sum(b[0, half : half + 2].astype(F32) for b in first)
    slot_load = load.astype(jnp.int32)[None]

    first_rows = jnp.concatenate([b[:, :half] for b in first], 0)
    second_rows = jnp.concatenate(second, 0)

    def up(which):
        w = w_in[0, which]
        return jnp.dot(first_rows, w[:half], preferred_element_type=F32) + jnp.dot(
            second_rows, w[half:], preferred_element_type=F32
        )

    hidden = (jax.nn.silu(up(0)) * up(1)).astype(BF16)
    place_of = {0: 0}
    for s in range(1, count // 2 + 1):
        place_of[count - s] = s
    for s in range(1, count // 2):
        place_of[s] = count // 2 + s
    down = [
        jnp.dot(hidden, w_down[0][:, :half], preferred_element_type=F32),
        jnp.dot(hidden, w_down[0][:, half:], preferred_element_type=F32),
    ]

    def block(c):
        return lambda s: down[c][place_of[s] * MOST : (place_of[s] + 1) * MOST]

    summed = jnp.concatenate(reduce_ring([block(0), block(1)], count), 1)

    mix = chosen.T * coef[:, None]
    mix_high = mix.astype(BF16)
    mix_low = (mix - mix_high.astype(F32)).astype(BF16)
    share = jnp.dot(mix_high, summed, preferred_element_type=F32) + jnp.dot(
        mix_low, summed, preferred_element_type=F32
    )
    near_count = peers * rows
    other = core_swap(share[near_count:].astype(BF16), groups)
    pair = (share[:near_count] + other.astype(F32)).astype(BF16)
    back = lax.all_to_all(
        pair.reshape(peers, rows, width), "expert", 0, 0, axis_index_groups=same_core, tiled=True
    )
    layer_output = jnp.sum(back.astype(F32), 0).astype(BF16)
    return layer_output, slot_load


def solution(mesh):
    placed = (
        P(("attn", "expert"), None),
        P(("attn", "expert"), None),
        P(("attn", "expert"), None),
        P(("attn", "expert"), None),
        P(),
        P("expert", None, None, "attn"),
        P("expert", "attn", None),
    )
    return jax.shard_map(
        body,
        mesh=mesh,
        in_specs=placed,
        out_specs=(P(("attn", "expert"), None), P("expert", None)),
        check_vma=False,
    )
```

```python
import functools

import jax
import jax.numpy as jnp
from jax import lax
from jax.experimental import pallas as pl
from jax.experimental.pallas import tpu as pltpu
from jax.sharding import PartitionSpec as P

F32, BF16 = jnp.float32, jnp.bfloat16
MOST = 24
META = 128
CHUNKS = 4
SUM_CHUNKS = 2


def core_swap(value, groups):
    return lax.ppermute(value, "expert", [(i, i ^ 1) for i in range(groups)])


def core_ring(value, sign, count, groups):
    pairs = []
    for a in range(count):
        for e in range(groups):
            step = sign if e % 2 == 0 else -sign
            pairs.append((a * groups + e, (a + step) % count * groups + e))
    return lax.ppermute(value, ("attn", "expert"), pairs)


def gather_ring(chunks, count, groups):
    half = count // 2
    moving = [[c] for c in chunks]
    for step in range(1, half + 1):
        for got in moving:
            sending = got[-1] if step < half else got[-1][:MOST]
            got.append(core_ring(sending, 1, count, groups))
    other = [
        core_swap(jnp.concatenate([b[MOST:] for b in got[1:half]], 0), groups) for got in moving
    ]
    return moving, other


def reduce_ring(chunks, count, groups):
    half = count // 2
    fore = [f(half).astype(BF16) for f in chunks]
    back = [f(count - half + 1).astype(BF16) for f in chunks]
    for step in range(half - 1, 0, -1):
        for c, f in enumerate(chunks):
            fore[c] = (core_ring(fore[c], 1, count, groups).astype(F32) + f(step)).astype(BF16)
            if step > 1:
                back[c] = (
                    core_ring(back[c], -1, count, groups).astype(F32) + f(count - step + 1)
                ).astype(BF16)
    return [
        (
            f(0)
            + core_ring(fore[c], 1, count, groups).astype(F32)
            + core_ring(back[c], -1, count, groups).astype(F32)
        ).astype(BF16)
        for c, f in enumerate(chunks)
    ]


def prep_kernel(top, *refs):
    sources, sent, held, sem = refs[:4], refs[4], refs[5:9], refs[9]
    copies = [pltpu.make_async_copy(s, h, sem.at[i]) for i, (s, h) in enumerate(zip(sources, held))]
    for copy in copies:
        copy.start()
    for copy in copies:
        copy.wait()
    tokens, ids, replica, weight = held
    rows, width = tokens.shape
    sent[:, :width] = tokens[...]
    high = weight[...].astype(BF16).astype(F32)
    middle = (weight[...] - high).astype(BF16).astype(F32)
    low = weight[...] - high - middle
    lane = lax.broadcasted_iota(jnp.int32, (rows, META), 1)
    meta = jnp.zeros((rows, META), F32)
    for part, value in enumerate([ids[...].astype(F32), replica[...].astype(F32), high, middle, low]):
        for k in range(top):
            meta = jnp.where(lane == part * top + k, value[:, k : k + 1], meta)
    sent[:, width:] = meta.astype(BF16)


def pack_kernel(top, span, near, far, plan, *outs):
    packed, mix, spare_plan, sem = outs[:CHUNKS], outs[CHUNKS], outs[CHUNKS + 1], outs[CHUNKS + 2]
    plan_copy = pltpu.make_async_copy(plan, spare_plan, sem)
    plan_copy.start()
    half = near.shape[0]
    total = 2 * half
    width = span * CHUNKS
    me = lax.axis_index("expert")
    info = jnp.concatenate([near[:, width:], far[:, width:]], 0)
    source = lax.broadcasted_iota(jnp.int32, (META, META), 0)
    lane = lax.broadcasted_iota(jnp.int32, (META, META), 1)

    def part(number):
        move = ((source == lane + number * top) & (lane < top)).astype(BF16)
        return jnp.dot(info, move, preferred_element_type=F32)

    ids, copies = part(0), part(1)
    weights = [part(2), part(3), part(4)]
    valid = lax.broadcasted_iota(jnp.int32, (total, META), 1) < top
    ones = jnp.ones((8, META), BF16)

    def along(value):
        return lax.dot_general(
            ones, value.astype(BF16), (((1,), (1,)), ((), ())), preferred_element_type=F32
        )

    turn = jnp.where(me % 2 == 0, 0, half)
    first = lax.broadcasted_iota(jnp.int32, (total, total), 0)
    second = lax.broadcasted_iota(jnp.int32, (total, total), 1)
    earlier = ((first + turn) % total < (second + turn) % total).astype(BF16)
    slot = lax.broadcasted_iota(jnp.int32, (MOST, total), 0).astype(F32)
    tail_lane = lax.broadcasted_iota(jnp.int32, (MOST, META), 1)
    chosen, tails = [], []
    plan_copy.wait()
    for which in range(2):
        expert = me if which == 0 else me ^ 1
        named = valid & (ids == expert.astype(F32))
        spare = spare_plan[expert].astype(F32)
        hit = along(named.astype(F32))
        rank = jnp.dot(hit.astype(BF16), earlier, preferred_element_type=F32)
        pick = jnp.where((hit[:1] > 0.0) & (rank[:1] == slot), 1.0, 0.0)
        chosen.append(pick)
        own_count = jnp.sum((named & (copies == 0.0)).astype(F32))
        spare_hit = valid & (ids == spare) & (copies == 1.0)
        spare_count = jnp.sum(spare_hit.astype(F32))
        tails.append(
            jnp.where(tail_lane == 0, own_count, jnp.where(tail_lane == 1, spare_count, 0.0))
        )
        if which == 0:
            coef = sum(along(jnp.where(named, w, 0.0)) for w in weights)
            value = pick * coef[:1]
            high = value.astype(BF16)
            mix[0] = high
            mix[1] = (value - high.astype(F32)).astype(BF16)
    pick = jnp.concatenate(chosen, 0).astype(BF16)
    for c in range(CHUNKS):
        at = slice(c * span, (c + 1) * span)
        value = jnp.dot(pick[:, :half], near[:, at], preferred_element_type=F32)
        value += jnp.dot(pick[:, half:], far[:, at], preferred_element_type=F32)
        packed[c][:, :span] = value.astype(BF16)
    packed[0][:, span:] = jnp.concatenate(tails, 0).astype(BF16)


def body(tokens, expert_ids, replica, route_weight, spare_plan, w_in, w_down):
    rows, width = tokens.shape
    top = expert_ids.shape[1]
    count = lax.axis_size("attn")
    groups = lax.axis_size("expert")
    peers = groups // 2
    half = count // 2
    same_core = [[core + 2 * j for j in range(peers)] for core in range(2)]
    vmem, anywhere = pl.BlockSpec(memory_space=pltpu.VMEM), pl.BlockSpec(memory_space=pltpu.HBM)
    routed = (tokens, expert_ids, replica, route_weight)
    grant = pltpu.CompilerParams(vmem_limit_bytes=16 * 2**20)

    sent = pl.pallas_call(
        functools.partial(prep_kernel, top),
        out_shape=jax.ShapeDtypeStruct((rows, width + META), BF16),
        in_specs=[anywhere] * 4,
        out_specs=vmem,
        scratch_shapes=[pltpu.VMEM(v.shape, v.dtype) for v in routed]
        + [pltpu.SemaphoreType.DMA((4,))],
        compiler_params=grant,
    )(*routed)

    spread = jnp.broadcast_to(sent[None], (peers, rows, width + META))
    near = lax.all_to_all(spread, "expert", 0, 0, axis_index_groups=same_core, tiled=True)
    near = lax.optimization_barrier(near.reshape(peers * rows, width + META))
    far = core_swap(near, groups)
    total = 2 * peers * rows

    span = width // CHUNKS
    cols = [slice(c * span, (c + 1) * span) for c in range(CHUNKS)]
    shapes = [
        jax.ShapeDtypeStruct((2 * MOST, span + (META if c == 0 else 0)), BF16)
        for c in range(CHUNKS)
    ]
    *parts, mix = pl.pallas_call(
        functools.partial(pack_kernel, top, span),
        out_shape=shapes + [jax.ShapeDtypeStruct((2, MOST, total), BF16)],
        in_specs=[vmem, vmem, anywhere],
        out_specs=[vmem] * (CHUNKS + 1),
        scratch_shapes=[
            pltpu.SMEM(spare_plan.shape, spare_plan.dtype), pltpu.SemaphoreType.DMA(())
        ],
        compiler_params=grant,
    )(near, far, spare_plan)

    moving, other = gather_ring(parts, count, groups)

    load = sum(b[0, span : span + 2].astype(F32) for b in moving[0])
    load += jnp.sum(other[0].reshape(half - 1, MOST, -1)[:, 0, span : span + 2].astype(F32), 0)
    slot_load = load.astype(jnp.int32)[None]

    gathered = [
        jnp.concatenate([b[:MOST, :span] for b in got] + [handed[:, :span]], 0)
        for got, handed in zip(moving, other)
    ]

    def up(which):
        return sum(
            jnp.dot(x, w_in[0, which, cols[c]], preferred_element_type=F32)
            for c, x in enumerate(gathered)
        )

    hidden = (jax.nn.silu(up(0)) * up(1)).astype(BF16)
    place_of = {0: 0}
    for s in range(1, half + 1):
        place_of[count - s] = s
    for s in range(1, half):
        place_of[s] = half + s
    wide = width // SUM_CHUNKS
    down = [
        jnp.dot(
            hidden, w_down[0][:, c * wide : (c + 1) * wide], preferred_element_type=F32
        )
        for c in range(SUM_CHUNKS)
    ]

    def block(c):
        return lambda s: down[c][place_of[s] * MOST : (place_of[s] + 1) * MOST]

    summed = jnp.concatenate(
        reduce_ring([block(c) for c in range(SUM_CHUNKS)], count, groups), 1
    )

    share = sum(
        lax.dot_general(mix[i], summed, (((0,), (0,)), ((), ())), preferred_element_type=F32)
        for i in range(2)
    )
    near_count = peers * rows
    swapped = core_swap(share[near_count:].astype(BF16), groups)
    both = (share[:near_count] + swapped.astype(F32)).astype(BF16)
    back = lax.all_to_all(
        both.reshape(peers, rows, width), "expert", 0, 0, axis_index_groups=same_core, tiled=True
    )
    layer_output = jnp.sum(back.astype(F32), 0).astype(BF16)
    return layer_output, slot_load


def solution(mesh):
    placed = (
        P(("attn", "expert"), None),
        P(("attn", "expert"), None),
        P(("attn", "expert"), None),
        P(("attn", "expert"), None),
        P(),
        P("expert", None, None, "attn"),
        P("expert", "attn", None),
    )
    return jax.shard_map(
        body,
        mesh=mesh,
        in_specs=placed,
        out_specs=(P(("attn", "expert"), None), P("expert", None)),
        check_vma=False,
    )
```

```python
import functools

import jax
import jax.numpy as jnp
from jax import lax
from jax.experimental import pallas as pl
from jax.experimental.pallas import tpu as pltpu
from jax.sharding import PartitionSpec as P

F32, BF16 = jnp.float32, jnp.bfloat16
MOST = 24
META = 128
PREP_VMEM = 60 * 2**20
CHUNKS = 3
SUM_CHUNKS = 2


def core_swap(value, groups):
    return lax.ppermute(value, "expert", [(i, i ^ 1) for i in range(groups)])


def core_ring(value, sign, count, groups):
    pairs = []
    for a in range(count):
        for e in range(groups):
            step = sign if e % 2 == 0 else -sign
            pairs.append((a * groups + e, (a + step) % count * groups + e))
    return lax.ppermute(value, ("attn", "expert"), pairs)


def gather_ring(chunks, count, groups):
    half = count // 2
    moving = [[c] for c in chunks]
    for step in range(1, half + 1):
        for got in moving:
            sending = got[-1] if step < half else got[-1][:MOST]
            got.append(core_ring(sending, 1, count, groups))
    other = [
        core_swap(jnp.concatenate([b[MOST:] for b in got[1:half]], 0), groups) for got in moving
    ]
    return moving, other


def reduce_ring(chunks, count, groups):
    half = count // 2
    fore = [f(half).astype(BF16) for f in chunks]
    back = [f(count - half + 1).astype(BF16) for f in chunks]
    for step in range(half - 1, 0, -1):
        for c, f in enumerate(chunks):
            fore[c] = (core_ring(fore[c], 1, count, groups).astype(F32) + f(step)).astype(BF16)
            if step > 1:
                back[c] = (
                    core_ring(back[c], -1, count, groups).astype(F32) + f(count - step + 1)
                ).astype(BF16)
            fore[c], back[c] = lax.optimization_barrier((fore[c], back[c]))
    return [
        (
            f(0)
            + core_ring(fore[c], 1, count, groups).astype(F32)
            + core_ring(back[c], -1, count, groups).astype(F32)
        ).astype(BF16)
        for c, f in enumerate(chunks)
    ]


def prep_kernel(top, *refs):
    sources, spread, held, sem = refs[:5], refs[5], refs[6:11], refs[11]
    copies = [pltpu.make_async_copy(s, h, sem.at[i]) for i, (s, h) in enumerate(zip(sources, held))]
    for copy in copies:
        copy.start()
    for copy in copies:
        copy.wait()
    tokens, ids, replica, weight, plan = held
    rows, width = tokens.shape
    high = weight[...].astype(BF16).astype(F32)
    middle = (weight[...] - high).astype(BF16).astype(F32)
    low = weight[...] - high - middle
    host = jnp.zeros(ids.shape, jnp.int32)
    for index in range(plan.shape[0]):
        host = jnp.where(ids[...] == plan[index], index, host)
    parts = [ids[...].astype(F32), replica[...].astype(F32), high, middle, low, host.astype(F32)]
    lane = lax.broadcasted_iota(jnp.int32, (rows, META), 1)
    meta = jnp.zeros((rows, META), F32)
    for part, value in enumerate(parts):
        for k in range(top):
            meta = jnp.where(lane == part * top + k, value[:, k : k + 1], meta)
    meta = meta.astype(BF16)
    for peer in range(spread.shape[0]):
        spread[peer, :, :width] = tokens[...]
        spread[peer, :, width:] = meta


def pack_kernel(top, cols, near, far, *outs):
    packed, mix = outs[:CHUNKS], outs[CHUNKS]
    half = near.shape[0]
    total = 2 * half
    width = cols[-1].stop
    me = lax.axis_index("expert")
    info = jnp.concatenate([near[:, width:], far[:, width:]], 0)
    source = lax.broadcasted_iota(jnp.int32, (META, META), 0)
    lane = lax.broadcasted_iota(jnp.int32, (META, META), 1)

    def part(number):
        move = ((source == lane + number * top) & (lane < top)).astype(BF16)
        return jnp.dot(info, move, preferred_element_type=F32)

    ids, copies, hosts = part(0), part(1), part(5)
    weights = [part(2), part(3), part(4)]
    valid = lax.broadcasted_iota(jnp.int32, (total, META), 1) < top
    ones = jnp.ones((8, META), BF16)

    def along(value):
        return lax.dot_general(
            ones, value.astype(BF16), (((1,), (1,)), ((), ())), preferred_element_type=F32
        )

    turn = jnp.where(me % 2 == 0, 0, half)
    first = lax.broadcasted_iota(jnp.int32, (total, total), 0)
    second = lax.broadcasted_iota(jnp.int32, (total, total), 1)
    earlier = ((first + turn) % total < (second + turn) % total).astype(BF16)
    slot = lax.broadcasted_iota(jnp.int32, (MOST, total), 0).astype(F32)
    tail_lane = lax.broadcasted_iota(jnp.int32, (MOST, META), 1)
    chosen, tails = [], []
    for which in range(2):
        expert = me if which == 0 else me ^ 1
        named = valid & (ids == expert.astype(F32))
        hit = along(named.astype(F32))
        rank = jnp.dot(hit.astype(BF16), earlier, preferred_element_type=F32)
        pick = jnp.where((hit[:1] > 0.0) & (rank[:1] == slot), 1.0, 0.0)
        chosen.append(pick)
        own_count = jnp.sum((named & (copies == 0.0)).astype(F32))
        spare_hit = valid & (hosts == expert.astype(F32)) & (copies == 1.0)
        spare_count = jnp.sum(spare_hit.astype(F32))
        tails.append(
            jnp.where(tail_lane == 0, own_count, jnp.where(tail_lane == 1, spare_count, 0.0))
        )
        if which == 0:
            coef = sum(along(jnp.where(named, w, 0.0)) for w in weights)
            value = pick * coef[:1]
            high = value.astype(BF16)
            mix[0] = high
            mix[1] = (value - high.astype(F32)).astype(BF16)
    pick = jnp.concatenate(chosen, 0).astype(BF16)
    tail = jnp.concatenate(tails, 0).astype(BF16)
    for out, at in zip(packed, cols):
        value = jnp.dot(pick[:, :half], near[:, at], preferred_element_type=F32)
        value += jnp.dot(pick[:, half:], far[:, at], preferred_element_type=F32)
        out[:, : at.stop - at.start] = value.astype(BF16)
    packed[-1][:, cols[-1].stop - cols[-1].start :] = tail


def body(tokens, expert_ids, replica, route_weight, spare_plan, w_in, w_down):
    rows, width = tokens.shape
    top = expert_ids.shape[1]
    count = lax.axis_size("attn")
    groups = lax.axis_size("expert")
    peers = groups // 2
    half = count // 2
    same_core = [[core + 2 * j for j in range(peers)] for core in range(2)]
    vmem, anywhere = pl.BlockSpec(memory_space=pltpu.VMEM), pl.BlockSpec(memory_space=pltpu.HBM)
    routed = (tokens, expert_ids, replica, route_weight)
    grant = pltpu.CompilerParams(vmem_limit_bytes=16 * 2**20)

    spread = pl.pallas_call(
        functools.partial(prep_kernel, top),
        out_shape=jax.ShapeDtypeStruct((peers, rows, width + META), BF16),
        in_specs=[anywhere] * 5,
        out_specs=vmem,
        scratch_shapes=[pltpu.VMEM(v.shape, v.dtype) for v in routed]
        + [pltpu.SMEM(spare_plan.shape, spare_plan.dtype), pltpu.SemaphoreType.DMA((5,))],
        compiler_params=pltpu.CompilerParams(vmem_limit_bytes=PREP_VMEM),
    )(*routed, spare_plan)

    near = lax.all_to_all(spread, "expert", 0, 0, axis_index_groups=same_core, tiled=True)
    near = lax.optimization_barrier(near.reshape(peers * rows, width + META))
    far = core_swap(near, groups)
    total = 2 * peers * rows

    span = (width + META) // CHUNKS
    cols = [slice(c * span, min((c + 1) * span, width)) for c in range(CHUNKS)]
    last = cols[-1].stop - cols[-1].start
    shapes = [
        jax.ShapeDtypeStruct((2 * MOST, span), BF16)
        for c in range(CHUNKS)
    ]
    *parts, mix = pl.pallas_call(
        functools.partial(pack_kernel, top, cols),
        out_shape=shapes + [jax.ShapeDtypeStruct((2, MOST, total), BF16)],
        in_specs=[vmem] * 2,
        out_specs=[vmem] * (CHUNKS + 1),
        compiler_params=grant,
    )(near, far)

    moving, other = gather_ring(parts, count, groups)

    counts = slice(last, last + 2)
    load = sum(b[0, counts].astype(F32) for b in moving[-1])
    load += jnp.sum(other[-1].reshape(half - 1, MOST, span)[:, 0, counts].astype(F32), 0)
    slot_load = load.astype(jnp.int32)[None]

    gathered = [
        jnp.concatenate([b[:, : at.stop - at.start] for b in [got[0][:MOST]] + [v[:MOST] for v in got[1:]] + [handed]], 0)
        for got, handed, at in zip(moving, other, cols)
    ]

    def up(which):
        return sum(
            jnp.dot(x, w_in[0, which, cols[c]], preferred_element_type=F32)
            for c, x in reversed(list(enumerate(gathered)))
        )

    hidden = (jax.nn.silu(up(0)) * up(1)).astype(BF16)
    place_of = {0: 0}
    for s in range(1, half + 1):
        place_of[count - s] = s
    for s in range(1, half):
        place_of[s] = half + s
    wide = width // SUM_CHUNKS
    down = [
        jnp.dot(
            hidden, w_down[0][:, c * wide : (c + 1) * wide], preferred_element_type=F32
        )
        for c in range(SUM_CHUNKS)
    ]

    def block(c):
        return lambda s: down[c][place_of[s] * MOST : (place_of[s] + 1) * MOST]

    summed = jnp.concatenate(
        reduce_ring([block(c) for c in range(SUM_CHUNKS)], count, groups), 1
    )

    share = sum(
        lax.dot_general(mix[i], summed, (((0,), (0,)), ((), ())), preferred_element_type=F32)
        for i in range(2)
    )
    near_count = peers * rows
    swapped = core_swap(share[near_count:].astype(BF16), groups)
    both = (share[:near_count] + swapped.astype(F32)).astype(BF16)
    back = lax.all_to_all(
        both.reshape(peers, rows, width), "expert", 0, 0, axis_index_groups=same_core, tiled=True
    )
    layer_output = jnp.sum(back.astype(F32), 0).astype(BF16)
    return layer_output, slot_load


def solution(mesh):
    placed = (
        P(("attn", "expert"), None),
        P(("attn", "expert"), None),
        P(("attn", "expert"), None),
        P(("attn", "expert"), None),
        P(),
        P("expert", None, None, "attn"),
        P("expert", "attn", None),
    )
    return jax.shard_map(
        body,
        mesh=mesh,
        in_specs=placed,
        out_specs=(P(("attn", "expert"), None), P("expert", None)),
        check_vma=False,
    )
```

```python
import functools

import jax
import jax.numpy as jnp
from jax import lax
from jax.experimental import pallas as pl
from jax.experimental.pallas import tpu as pltpu
from jax.sharding import PartitionSpec as P

F32, BF16 = jnp.float32, jnp.bfloat16
MOST = 24
META = 128
PREP_VMEM = 60 * 2**20
CHUNKS = 3
TILE = 512
SUM_CHUNKS = 2


def core_swap(value, groups):
    return lax.ppermute(value, "expert", [(i, i ^ 1) for i in range(groups)])


def core_ring(value, sign, count, groups):
    pairs = []
    for a in range(count):
        for e in range(groups):
            step = sign if e % 2 == 0 else -sign
            pairs.append((a * groups + e, (a + step) % count * groups + e))
    return lax.ppermute(value, ("attn", "expert"), pairs)


def gather_ring(chunks, count, groups):
    half = count // 2
    moving = [[c] for c in chunks]
    for step in range(1, half + 1):
        for got in moving:
            sending = got[-1] if step < half else got[-1][:MOST]
            got.append(core_ring(sending, 1, count, groups))
    other = [
        core_swap(jnp.concatenate([b[MOST:] for b in got[1:half]], 0), groups) for got in moving
    ]
    return moving, other


def reduce_ring(chunks, count, groups):
    half = count // 2
    fore = [f(half).astype(BF16) for f in chunks]
    back = [f(count - half + 1).astype(BF16) for f in chunks]
    for step in range(half - 1, 0, -1):
        for c, f in enumerate(chunks):
            fore[c] = (core_ring(fore[c], 1, count, groups).astype(F32) + f(step)).astype(BF16)
            if step > 1:
                back[c] = (
                    core_ring(back[c], -1, count, groups).astype(F32) + f(count - step + 1)
                ).astype(BF16)
            fore[c], back[c] = lax.optimization_barrier((fore[c], back[c]))
    return [
        (
            f(0)
            + core_ring(fore[c], 1, count, groups).astype(F32)
            + core_ring(back[c], -1, count, groups).astype(F32)
        ).astype(BF16)
        for c, f in enumerate(chunks)
    ]


def prep_kernel(top, *refs):
    sources, spread, held, sem = refs[:5], refs[5], refs[6:11], refs[11]
    copies = [pltpu.make_async_copy(s, h, sem.at[i]) for i, (s, h) in enumerate(zip(sources, held))]
    for copy in copies:
        copy.start()
    for copy in copies:
        copy.wait()
    tokens, ids, replica, weight, plan = held
    rows, width = tokens.shape
    high = weight[...].astype(BF16).astype(F32)
    middle = (weight[...] - high).astype(BF16).astype(F32)
    low = weight[...] - high - middle
    host = jnp.zeros(ids.shape, jnp.int32)
    for index in range(plan.shape[0]):
        host = jnp.where(ids[...] == plan[index], index, host)
    parts = [ids[...].astype(F32), replica[...].astype(F32), high, middle, low, host.astype(F32)]
    lane = lax.broadcasted_iota(jnp.int32, (rows, META), 1)
    meta = jnp.zeros((rows, META), F32)
    for part, value in enumerate(parts):
        for k in range(top):
            meta = jnp.where(lane == part * top + k, value[:, k : k + 1], meta)
    meta = meta.astype(BF16)
    for peer in range(spread.shape[0]):
        spread[peer, :, :width] = tokens[...]
        spread[peer, :, width:] = meta


def pack_kernel(top, cols, near, far, *outs):
    packed, mix = outs[:CHUNKS], outs[CHUNKS]
    half = near.shape[0]
    total = 2 * half
    width = cols[-1].stop
    me = lax.axis_index("expert")
    info = jnp.concatenate([near[:, width:], far[:, width:]], 0)
    source = lax.broadcasted_iota(jnp.int32, (META, META), 0)
    lane = lax.broadcasted_iota(jnp.int32, (META, META), 1)

    def part(number):
        move = ((source == lane + number * top) & (lane < top)).astype(BF16)
        return jnp.dot(info, move, preferred_element_type=F32)

    ids, copies, hosts = part(0), part(1), part(5)
    weights = [part(2), part(3), part(4)]
    valid = lax.broadcasted_iota(jnp.int32, (total, META), 1) < top
    ones = jnp.ones((8, META), BF16)

    def along(value):
        return lax.dot_general(
            ones, value.astype(BF16), (((1,), (1,)), ((), ())), preferred_element_type=F32
        )

    turn = jnp.where(me % 2 == 0, 0, half)
    first = lax.broadcasted_iota(jnp.int32, (total, total), 0)
    second = lax.broadcasted_iota(jnp.int32, (total, total), 1)
    earlier = ((first + turn) % total < (second + turn) % total).astype(BF16)
    slot = lax.broadcasted_iota(jnp.int32, (MOST, total), 0).astype(F32)
    tail_lane = lax.broadcasted_iota(jnp.int32, (MOST, META), 1)
    chosen, tails = [], []
    for which in range(2):
        expert = me if which == 0 else me ^ 1
        named = valid & (ids == expert.astype(F32))
        hit = along(named.astype(F32))
        rank = jnp.dot(hit.astype(BF16), earlier, preferred_element_type=F32)
        pick = jnp.where((hit[:1] > 0.0) & (rank[:1] == slot), 1.0, 0.0)
        chosen.append(pick)
        own_count = jnp.sum((named & (copies == 0.0)).astype(F32))
        spare_hit = valid & (hosts == expert.astype(F32)) & (copies == 1.0)
        spare_count = jnp.sum(spare_hit.astype(F32))
        tails.append(
            jnp.where(tail_lane == 0, own_count, jnp.where(tail_lane == 1, spare_count, 0.0))
        )
        if which == 0:
            coef = sum(along(jnp.where(named, w, 0.0)) for w in weights)
            value = pick * coef[:1]
            high = value.astype(BF16)
            mix[0] = high
            mix[1] = (value - high.astype(F32)).astype(BF16)
    pick = jnp.concatenate(chosen, 0).astype(BF16)
    tail = jnp.concatenate(tails, 0).astype(BF16)
    for out, at in zip(packed, cols):
        value = jnp.dot(pick[:, :half], near[:, at], preferred_element_type=F32)
        value += jnp.dot(pick[:, half:], far[:, at], preferred_element_type=F32)
        out[:, : at.stop - at.start] = value.astype(BF16)
    packed[-1][:, cols[-1].stop - cols[-1].start :] = tail


def mix_kernel(near, mix, *refs):
    chunks, mine, theirs = refs[:-2], refs[-2], refs[-1]
    at = 0
    for chunk in chunks:
        for k in range(0, chunk.shape[1], TILE):
            value = sum(
                lax.dot_general(
                    mix[i], chunk[:, k : k + TILE], (((0,), (0,)), ((), ())),
                    preferred_element_type=F32,
                )
                for i in range(2)
            )
            mine[:, at : at + TILE] = value[:near]
            theirs[:, at : at + TILE] = value[near:].astype(BF16)
            at += TILE


def close_kernel(mine, other, result):
    peers, rows, _ = result.shape
    for k in range(0, result.shape[2], TILE):
        value = (mine[:, k : k + TILE] + other[:, k : k + TILE].astype(F32)).astype(BF16)
        for peer in range(peers):
            result[peer, :, k : k + TILE] = value[peer * rows : (peer + 1) * rows]


def body(tokens, expert_ids, replica, route_weight, spare_plan, w_in, w_down):
    rows, width = tokens.shape
    top = expert_ids.shape[1]
    count = lax.axis_size("attn")
    groups = lax.axis_size("expert")
    peers = groups // 2
    half = count // 2
    same_core = [[core + 2 * j for j in range(peers)] for core in range(2)]
    vmem, anywhere = pl.BlockSpec(memory_space=pltpu.VMEM), pl.BlockSpec(memory_space=pltpu.HBM)
    routed = (tokens, expert_ids, replica, route_weight)
    grant = pltpu.CompilerParams(vmem_limit_bytes=16 * 2**20)

    spread = pl.pallas_call(
        functools.partial(prep_kernel, top),
        out_shape=jax.ShapeDtypeStruct((peers, rows, width + META), BF16),
        in_specs=[anywhere] * 5,
        out_specs=vmem,
        scratch_shapes=[pltpu.VMEM(v.shape, v.dtype) for v in routed]
        + [pltpu.SMEM(spare_plan.shape, spare_plan.dtype), pltpu.SemaphoreType.DMA((5,))],
        compiler_params=pltpu.CompilerParams(vmem_limit_bytes=PREP_VMEM),
    )(*routed, spare_plan)

    near = lax.all_to_all(spread, "expert", 0, 0, axis_index_groups=same_core, tiled=True)
    near = lax.optimization_barrier(near.reshape(peers * rows, width + META))
    far = core_swap(near, groups)
    total = 2 * peers * rows

    span = (width + META) // CHUNKS
    cols = [slice(c * span, min((c + 1) * span, width)) for c in range(CHUNKS)]
    last = cols[-1].stop - cols[-1].start
    shapes = [
        jax.ShapeDtypeStruct((2 * MOST, span), BF16)
        for c in range(CHUNKS)
    ]
    *parts, mix = pl.pallas_call(
        functools.partial(pack_kernel, top, cols),
        out_shape=shapes + [jax.ShapeDtypeStruct((2, MOST, total), BF16)],
        in_specs=[vmem] * 2,
        out_specs=[vmem] * (CHUNKS + 1),
        compiler_params=grant,
    )(near, far)

    moving, other = gather_ring(parts, count, groups)

    counts = slice(last, last + 2)
    load = sum(b[0, counts].astype(F32) for b in moving[-1])
    load += jnp.sum(other[-1].reshape(half - 1, MOST, span)[:, 0, counts].astype(F32), 0)
    slot_load = load.astype(jnp.int32)[None]

    gathered = [
        jnp.concatenate([b[:, : at.stop - at.start] for b in [got[0][:MOST]] + [v[:MOST] for v in got[1:]] + [handed]], 0)
        for got, handed, at in zip(moving, other, cols)
    ]

    def up(which):
        return sum(
            jnp.dot(x, w_in[0, which, cols[c]], preferred_element_type=F32)
            for c, x in reversed(list(enumerate(gathered)))
        )

    hidden = (jax.nn.silu(up(0)) * up(1)).astype(BF16)
    place_of = {0: 0}
    for s in range(1, half + 1):
        place_of[count - s] = s
    for s in range(1, half):
        place_of[s] = half + s
    wide = width // SUM_CHUNKS
    down = [
        jnp.dot(
            hidden, w_down[0][:, c * wide : (c + 1) * wide], preferred_element_type=F32
        )
        for c in range(SUM_CHUNKS)
    ]

    def block(c):
        return lambda s: down[c][place_of[s] * MOST : (place_of[s] + 1) * MOST]

    sums = reduce_ring([block(c) for c in range(SUM_CHUNKS)], count, groups)

    near_count = peers * rows
    mine, theirs = pl.pallas_call(
        functools.partial(mix_kernel, near_count),
        out_shape=[
            jax.ShapeDtypeStruct((near_count, width), F32),
            jax.ShapeDtypeStruct((near_count, width), BF16),
        ],
        in_specs=[vmem] * (1 + SUM_CHUNKS),
        out_specs=[vmem] * 2,
        compiler_params=grant,
    )(mix, *sums)
    both = pl.pallas_call(
        close_kernel,
        out_shape=jax.ShapeDtypeStruct((peers, rows, width), BF16),
        in_specs=[vmem] * 2,
        out_specs=vmem,
        compiler_params=grant,
    )(mine, core_swap(theirs, groups))
    back = lax.all_to_all(
        both, "expert", 0, 0, axis_index_groups=same_core, tiled=True
    )
    layer_output = jnp.sum(back.astype(F32), 0).astype(BF16)
    return layer_output, slot_load


def solution(mesh):
    placed = (
        P(("attn", "expert"), None),
        P(("attn", "expert"), None),
        P(("attn", "expert"), None),
        P(("attn", "expert"), None),
        P(),
        P("expert", None, None, "attn"),
        P("expert", "attn", None),
    )
    return jax.shard_map(
        body,
        mesh=mesh,
        in_specs=placed,
        out_specs=(P(("attn", "expert"), None), P("expert", None)),
        check_vma=False,
    )
```

```python
import functools

import jax
import jax.numpy as jnp
from jax import lax
from jax.experimental import pallas as pl
from jax.experimental.pallas import tpu as pltpu
from jax.sharding import PartitionSpec as P

F32, BF16 = jnp.float32, jnp.bfloat16
MOST = 24
META = 128
PREP_VMEM = 60 * 2**20
CHUNKS = 3
SUM_CHUNKS = 2


def core_swap(value, groups):
    return lax.ppermute(value, "expert", [(i, i ^ 1) for i in range(groups)])


def core_ring(value, sign, count, groups):
    pairs = []
    for a in range(count):
        for e in range(groups):
            step = sign if e % 2 == 0 else -sign
            pairs.append((a * groups + e, (a + step) % count * groups + e))
    return lax.ppermute(value, ("attn", "expert"), pairs)


def gather_ring(chunks, count, groups):
    half = count // 2
    moving = [[c] for c in chunks]
    for step in range(1, half + 1):
        for got in moving:
            sending = got[-1] if step < half else got[-1][:MOST]
            got.append(core_ring(sending, 1, count, groups))
    other = [
        core_swap(jnp.concatenate([b[MOST:] for b in got[1:half]], 0), groups) for got in moving
    ]
    return moving, other


def reduce_ring(chunks, count, groups):
    half = count // 2
    fore = [f(half).astype(BF16) for f in chunks]
    back = [f(count - half + 1).astype(BF16) for f in chunks]
    for step in range(half - 1, 0, -1):
        for c, f in enumerate(chunks):
            fore[c] = (core_ring(fore[c], 1, count, groups).astype(F32) + f(step)).astype(BF16)
            if step > 1:
                back[c] = (
                    core_ring(back[c], -1, count, groups).astype(F32) + f(count - step + 1)
                ).astype(BF16)
            fore[c], back[c] = lax.optimization_barrier((fore[c], back[c]))
    return [
        (
            f(0)
            + core_ring(fore[c], 1, count, groups).astype(F32)
            + core_ring(back[c], -1, count, groups).astype(F32)
        ).astype(BF16)
        for c, f in enumerate(chunks)
    ]


def prep_kernel(top, *refs):
    sources, spread, held, sem = refs[:5], refs[5], refs[6:11], refs[11]
    copies = [pltpu.make_async_copy(s, h, sem.at[i]) for i, (s, h) in enumerate(zip(sources, held))]
    for copy in copies:
        copy.start()
    for copy in copies:
        copy.wait()
    tokens, ids, replica, weight, plan = held
    rows, width = tokens.shape
    high = weight[...].astype(BF16).astype(F32)
    middle = (weight[...] - high).astype(BF16).astype(F32)
    low = weight[...] - high - middle
    host = jnp.zeros(ids.shape, jnp.int32)
    for index in range(plan.shape[0]):
        host = jnp.where(ids[...] == plan[index], index, host)
    parts = [ids[...].astype(F32), replica[...].astype(F32), high, middle, low, host.astype(F32)]
    lane = lax.broadcasted_iota(jnp.int32, (rows, META), 1)
    meta = jnp.zeros((rows, META), F32)
    for part, value in enumerate(parts):
        for k in range(top):
            meta = jnp.where(lane == part * top + k, value[:, k : k + 1], meta)
    meta = meta.astype(BF16)
    for peer in range(spread.shape[0]):
        spread[peer, :, :width] = tokens[...]
        spread[peer, :, width:] = meta


def pack_kernel(top, cols, near, far, *outs):
    packed, mix = outs[:CHUNKS], outs[CHUNKS]
    half = near.shape[0]
    total = 2 * half
    width = cols[-1].stop
    me = lax.axis_index("expert")
    info = jnp.concatenate([near[:, width:], far[:, width:]], 0)
    source = lax.broadcasted_iota(jnp.int32, (META, META), 0)
    lane = lax.broadcasted_iota(jnp.int32, (META, META), 1)

    def part(number):
        move = ((source == lane + number * top) & (lane < top)).astype(BF16)
        return jnp.dot(info, move, preferred_element_type=F32)

    ids, copies, hosts = part(0), part(1), part(5)
    weights = [part(2), part(3), part(4)]
    valid = lax.broadcasted_iota(jnp.int32, (total, META), 1) < top
    ones = jnp.ones((8, META), BF16)

    def along(value):
        return lax.dot_general(
            ones, value.astype(BF16), (((1,), (1,)), ((), ())), preferred_element_type=F32
        )

    turn = jnp.where(me % 2 == 0, 0, half)
    first = lax.broadcasted_iota(jnp.int32, (total, total), 0)
    second = lax.broadcasted_iota(jnp.int32, (total, total), 1)
    earlier = ((first + turn) % total < (second + turn) % total).astype(BF16)
    slot = lax.broadcasted_iota(jnp.int32, (MOST, total), 0).astype(F32)
    tail_lane = lax.broadcasted_iota(jnp.int32, (MOST, META), 1)
    chosen, tails = [], []
    for which in range(2):
        expert = me if which == 0 else me ^ 1
        named = valid & (ids == expert.astype(F32))
        hit = along(named.astype(F32))
        rank = jnp.dot(hit.astype(BF16), earlier, preferred_element_type=F32)
        pick = jnp.where((hit[:1] > 0.0) & (rank[:1] == slot), 1.0, 0.0)
        chosen.append(pick)
        own_count = jnp.sum((named & (copies == 0.0)).astype(F32))
        spare_hit = valid & (hosts == expert.astype(F32)) & (copies == 1.0)
        spare_count = jnp.sum(spare_hit.astype(F32))
        tails.append(
            jnp.where(tail_lane == 0, own_count, jnp.where(tail_lane == 1, spare_count, 0.0))
        )
        if which == 0:
            coef = sum(along(jnp.where(named, w, 0.0)) for w in weights)
            value = pick * coef[:1]
            high = value.astype(BF16)
            mix[0] = high
            mix[1] = (value - high.astype(F32)).astype(BF16)
    pick = jnp.concatenate(chosen, 0).astype(BF16)
    tail = jnp.concatenate(tails, 0).astype(BF16)
    for out, at in zip(packed, cols):
        value = jnp.dot(pick[:, :half], near[:, at], preferred_element_type=F32)
        value += jnp.dot(pick[:, half:], far[:, at], preferred_element_type=F32)
        out[:, : at.stop - at.start] = value.astype(BF16)
    packed[-1][:, cols[-1].stop - cols[-1].start :] = tail


def up_kernel(cols, w, *refs):
    acc = 0.0
    for x, at in zip(refs[:-1], cols):
        both = jnp.concatenate([w[0, 0, at, :], w[0, 1, at, :]], 1)
        acc += jnp.dot(x[...], both, preferred_element_type=F32)
    ff = w.shape[3]
    refs[-1][...] = (jax.nn.silu(acc[:, :ff]) * acc[:, ff:]).astype(BF16)


def body(tokens, expert_ids, replica, route_weight, spare_plan, w_in, w_down):
    rows, width = tokens.shape
    top = expert_ids.shape[1]
    count = lax.axis_size("attn")
    groups = lax.axis_size("expert")
    peers = groups // 2
    half = count // 2
    same_core = [[core + 2 * j for j in range(peers)] for core in range(2)]
    vmem, anywhere = pl.BlockSpec(memory_space=pltpu.VMEM), pl.BlockSpec(memory_space=pltpu.HBM)
    routed = (tokens, expert_ids, replica, route_weight)
    grant = pltpu.CompilerParams(vmem_limit_bytes=16 * 2**20)

    spread = pl.pallas_call(
        functools.partial(prep_kernel, top),
        out_shape=jax.ShapeDtypeStruct((peers, rows, width + META), BF16),
        in_specs=[anywhere] * 5,
        out_specs=vmem,
        scratch_shapes=[pltpu.VMEM(v.shape, v.dtype) for v in routed]
        + [pltpu.SMEM(spare_plan.shape, spare_plan.dtype), pltpu.SemaphoreType.DMA((5,))],
        compiler_params=pltpu.CompilerParams(vmem_limit_bytes=PREP_VMEM),
    )(*routed, spare_plan)

    near = lax.all_to_all(spread, "expert", 0, 0, axis_index_groups=same_core, tiled=True)
    near = lax.optimization_barrier(near.reshape(peers * rows, width + META))
    far = core_swap(near, groups)
    total = 2 * peers * rows

    span = (width + META) // CHUNKS
    cols = [slice(c * span, min((c + 1) * span, width)) for c in range(CHUNKS)]
    last = cols[-1].stop - cols[-1].start
    shapes = [
        jax.ShapeDtypeStruct((2 * MOST, span), BF16)
        for c in range(CHUNKS)
    ]
    *parts, mix = pl.pallas_call(
        functools.partial(pack_kernel, top, cols),
        out_shape=shapes + [jax.ShapeDtypeStruct((2, MOST, total), BF16)],
        in_specs=[vmem] * 2,
        out_specs=[vmem] * (CHUNKS + 1),
        compiler_params=grant,
    )(near, far)

    moving, other = gather_ring(parts, count, groups)

    counts = slice(last, last + 2)
    load = sum(b[0, counts].astype(F32) for b in moving[-1])
    load += jnp.sum(other[-1].reshape(half - 1, MOST, span)[:, 0, counts].astype(F32), 0)
    slot_load = load.astype(jnp.int32)[None]

    gathered = [
        jnp.concatenate([b[:, : at.stop - at.start] for b in [got[0][:MOST]] + [v[:MOST] for v in got[1:]] + [handed]], 0)
        for got, handed, at in zip(moving, other, cols)
    ]

    hidden = pl.pallas_call(
        functools.partial(up_kernel, cols),
        out_shape=jax.ShapeDtypeStruct((count * MOST, w_in.shape[3]), BF16),
        in_specs=[vmem] * (1 + CHUNKS),
        out_specs=vmem,
        compiler_params=grant,
    )(w_in, *gathered)
    place_of = {0: 0}
    for s in range(1, half + 1):
        place_of[count - s] = s
    for s in range(1, half):
        place_of[s] = half + s
    wide = width // SUM_CHUNKS
    down = [
        jnp.dot(
            hidden, w_down[0][:, c * wide : (c + 1) * wide], preferred_element_type=F32
        )
        for c in range(SUM_CHUNKS)
    ]

    def block(c):
        return lambda s: down[c][place_of[s] * MOST : (place_of[s] + 1) * MOST]

    summed = jnp.concatenate(
        reduce_ring([block(c) for c in range(SUM_CHUNKS)], count, groups), 1
    )

    share = sum(
        lax.dot_general(mix[i], summed, (((0,), (0,)), ((), ())), preferred_element_type=F32)
        for i in range(2)
    )
    near_count = peers * rows
    swapped = core_swap(share[near_count:].astype(BF16), groups)
    both = (share[:near_count] + swapped.astype(F32)).astype(BF16)
    back = lax.all_to_all(
        both.reshape(peers, rows, width), "expert", 0, 0, axis_index_groups=same_core, tiled=True
    )
    layer_output = jnp.sum(back.astype(F32), 0).astype(BF16)
    return layer_output, slot_load


def solution(mesh):
    placed = (
        P(("attn", "expert"), None),
        P(("attn", "expert"), None),
        P(("attn", "expert"), None),
        P(("attn", "expert"), None),
        P(),
        P("expert", None, None, "attn"),
        P("expert", "attn", None),
    )
    return jax.shard_map(
        body,
        mesh=mesh,
        in_specs=placed,
        out_specs=(P(("attn", "expert"), None), P("expert", None)),
        check_vma=False,
    )
```
